32 devices in a mesh: dp: 4 (over x, core), blk: 4 (over z), resp: 2 (over y).
Axes of the slice: x: 2, y: 2, z: 4, core: 2. Of those that a mesh axis runs over, the one named last changes fastest.
Arguments:
- saved: bfloat16 [4, 512, 3, 1280], P('dp', 'blk', None, 'resp'), may hold values from -24 to 24
- prefix_cot: bfloat16 [4, 2, 512, 1280], P('dp', 'resp', 'blk'), may hold values from -24 to 24
- w_out: bfloat16 [1280, 1280], P('resp'), may hold values from -0.15625 to 0.15625
- lengths: int32 [4, 4], P('dp', 'resp'), may hold values from 1 to 512, 1024 in all within a row
- adv_mask: int32 [4, 4, 512], P('dp', 'resp'), may hold values from -3 to 3, as said below
- patch_map: int32 [4, 4, 128], P('dp', 'blk'), may hold values from 0 to 127, each once within a row
Outputs:
- grad_qkv: bfloat16 [4, 512, 3, 1280], P('dp', 'blk', None, 'resp')
The draws below stay inside these ranges and needn't reach their ends.
Inputs may be any that keep to these rules, and one draw needn't show every extreme that they name: `adv_mask`: within one response every nonzero entry has the same value. The 4 lengths of one image sum to 1024; the longest is 512. `patch_map`: each row of 128 entries holds every number of 0 to 127 once.
All inputs are finite; a program needn't handle non-finite values. No bound on the sum of `lengths` on one device may be relied on, other than what follows from the above.
Results may differ from the reference program's by a relative error of at most 0.03.
Values may be sent and summed in bfloat16 or wider, within the bound.
A program may use at most 64 MiB of HBM per device.

```python
import math
import jax
import jax.numpy as jnp
import numpy as np
from jax import lax

VD = 1280
HEADS = 16
HD = 80
PB = 128
MAXLEN = 512
RESP_DEV = 2
IMAGES = 4
BLOCKS = 4
GROUPS = 2
PATCHES = 512
RESPONSES = 4
LEN_TOTAL = 1024


def draw_saved(key, part):
    base_key = jax.random.fold_in(key, 0)
    data = jnp.clip(jax.random.normal(base_key, (IMAGES, PATCHES, 3, VD), jnp.float32), -4.0, 4.0) * 1.3
    return data.astype(jnp.bfloat16)


def draw_adv_mask(key, part):
    level_key, sign_key, mask_key = jax.random.split(key, 3)
    level = jax.random.randint(level_key, (IMAGES, RESPONSES, 1), 1, 4)
    sign = jax.random.randint(sign_key, (IMAGES, RESPONSES, 1), 0, 2) * 2 - 1
    marks = jax.random.randint(mask_key, (IMAGES, RESPONSES, MAXLEN), 0, 2)
    return (level * sign * marks).astype(jnp.int32)


def shard_levels(stream_key, dims, cuts, least, high):
    def one(dim, blocks):
        draws = jax.random.uniform(jax.random.fold_in(jax.random.fold_in(stream_key, 6), dim), (blocks,), jnp.float32, least / len(cuts), high / len(cuts))
        return jnp.repeat(jnp.exp(draws), dims[dim] // blocks).reshape((-1,) + (1,) * (len(dims) - dim - 1))

    gain = one(*cuts[0])
    for cut in cuts[1:]:
        gain = gain * one(*cut)
    return gain


def split_up(number_of, total, bound, lean):
    portions = [(1 << 20) // math.isqrt(standing ** lean) + 1 for standing in range(2, number_of + 1)]
    rest, holding = total - bound - (number_of - 1), [1] * (number_of - 1)
    while rest > 0:
        candidates = [i for i in range(number_of - 1) if holding[i] < bound]
        pool, budget = sum([portions[i] for i in candidates]), rest
        for i in candidates:
            extra = min(bound - holding[i], max(1, budget * portions[i] // pool), rest)
            holding[i] = holding[i] + extra
            rest = rest - extra
    return np.array([bound] + holding)


def ragged(key, number_of, total, bound, skew):
    if number_of == 2:
        one = jax.random.randint(key, (), max(1, total - bound), min(bound, total - 1) + 1)
        return jnp.stack([one, total - one])
    sizes = jnp.asarray(split_up(number_of, total, bound, skew), jnp.int32)
    pairs = (number_of - 1) // 2
    giver, receiver = sizes[1:1 + 2 * pairs:2], sizes[2:2 + 2 * pairs:2]
    room = jnp.minimum(giver - 1, bound - receiver)
    shifted = jax.random.randint(jax.random.fold_in(key, 1), (pairs,), 0, 1 << 20) % (room + 1)
    sizes = sizes.at[1:1 + 2 * pairs:2].set(giver - shifted).at[2:2 + 2 * pairs:2].set(receiver + shifted)
    return sizes[jax.random.permutation(jax.random.fold_in(key, 2), number_of)]


def bell_draw(own_key, shape, width, limit, cuts=(), kind=jnp.bfloat16):
    level = shard_levels(own_key, shape, cuts, -0.22, 0.18) if cuts else 1.0
    entries = jax.random.normal(own_key, shape, jnp.float32) * width * level
    return jnp.minimum(jnp.maximum(entries, -limit), limit).astype(kind)


def setup_inputs(seed: int = 0) -> dict:
    key_of = jax.random.split(jax.random.key(seed), 7)
    saved = draw_saved(jax.random.fold_in(key_of[6], 71), 0)
    prefix_cot = bell_draw(key_of[1], (IMAGES, GROUPS, PATCHES, VD), 4.0, 24.0, ((0, 4), (1, 2), (2, 4)))
    w_out = bell_draw(key_of[2], (VD, VD), VD ** -0.5, 0.15625, ((0, 2),))
    lengths = jax.vmap(lambda own: ragged(own, RESPONSES, LEN_TOTAL, MAXLEN, 2))(jax.random.split(key_of[3], IMAGES)).reshape((IMAGES, RESPONSES)).astype(jnp.int32)
    adv_mask = draw_adv_mask(jax.random.fold_in(key_of[6], 71), 0)
    patch_map = jax.vmap(lambda own: jax.random.permutation(own, PB))(jax.random.split(key_of[5], IMAGES * BLOCKS)).reshape((IMAGES, BLOCKS, PB)).astype(jnp.int32)
    return {"saved": saved, "prefix_cot": prefix_cot, "w_out": w_out, "lengths": lengths, "adv_mask": adv_mask, "patch_map": patch_map}


def one_head(item):
    query, keys, values, grad = item
    scale = 1.0 / math.sqrt(HD)
    score = jnp.dot(query, keys.T, preferred_element_type=jnp.float32) * scale
    top = lax.optimization_barrier(jnp.max(score, axis=1))
    expo = jnp.exp(score - top[:, None])
    row_total = lax.optimization_barrier(jnp.sum(expo, axis=1))
    output = (jnp.dot(expo.astype(jnp.bfloat16), values, preferred_element_type=jnp.float32) / row_total[:, None]).astype(jnp.bfloat16)
    log_total = top + jnp.log(row_total)
    delta = lax.optimization_barrier(jnp.sum(grad.astype(jnp.float32) * output.astype(jnp.float32), axis=1))
    prob = jnp.exp(score - log_total[:, None])
    prob_half = prob.astype(jnp.bfloat16)
    dprob = jnp.dot(grad, values.T, preferred_element_type=jnp.float32)
    dscore = (prob * (dprob - delta[:, None])).astype(jnp.bfloat16)
    grad_q = jnp.dot(dscore, keys, preferred_element_type=jnp.float32) * scale
    grad_k = jnp.dot(dscore.T, query, preferred_element_type=jnp.float32) * scale
    grad_v = jnp.dot(prob_half.T, grad, preferred_element_type=jnp.float32)
    return jnp.stack([grad_q, grad_k, grad_v]).astype(jnp.bfloat16)

def to_heads(x):
    return x.reshape(IMAGES, PATCHES, HEADS, HD).transpose(0, 2, 1, 3).reshape(IMAGES * HEADS, PATCHES, HD)

def reference(saved, prefix_cot, w_out, lengths, adv_mask, patch_map):
    live = jnp.arange(MAXLEN, dtype=jnp.int32)[None, None, :] < lengths[:, :, None]
    resp_weight = lax.optimization_barrier(jnp.sum(jnp.where(live, adv_mask, 0).astype(jnp.float32), axis=2)) / MAXLEN
    group_weight = lax.optimization_barrier(jnp.sum(resp_weight.reshape(IMAGES, GROUPS, RESP_DEV), axis=2))
    total = jnp.zeros((IMAGES, PATCHES, VD), jnp.float32)
    for group in range(GROUPS):
        total = total + group_weight[:, group, None, None] * prefix_cot[:, group].astype(jnp.float32)
    total = total.astype(jnp.bfloat16)
    index = (jnp.arange(BLOCKS, dtype=jnp.int32)[None, :, None] * PB + patch_map).reshape(IMAGES, PATCHES).astype(jnp.int32)
    cot_rows = jnp.take_along_axis(total, index[:, :, None], axis=1)
    grad_out = jnp.einsum('ipc,hc->iph', cot_rows.astype(jnp.float32), w_out.astype(jnp.float32)).astype(jnp.bfloat16)
    items = (to_heads(saved[:, :, 0, :]), to_heads(saved[:, :, 1, :]), to_heads(saved[:, :, 2, :]), to_heads(grad_out))
    result = lax.map(one_head, items)
    result = result.reshape(IMAGES, HEADS, 3, PATCHES, HD).transpose(0, 3, 2, 1, 4)
    return result.reshape(IMAGES, PATCHES, 3, VD)
```

```python
import functools
import math

import jax
import jax.numpy as jnp
from jax import lax
from jax.experimental import pallas as pl
from jax.experimental.pallas import tpu as pltpu
from jax.sharding import PartitionSpec as P

HD = 80
MAXLEN = 512
MESH = pl.DeviceIdType.MESH


def score_pair(query, grad, log_total, delta, keys, values, scale):
    score = jnp.einsum("qhd,khd->hqk", query, keys, preferred_element_type=jnp.float32) * scale
    prob = jnp.exp(score - log_total[:, :, None])
    dprob = jnp.einsum("qhd,khd->hqk", grad, values, preferred_element_type=jnp.float32)
    dscore = (prob * (dprob - delta[:, :, None])).astype(jnp.bfloat16)
    return (prob.astype(jnp.bfloat16), dscore)


def gathered(saved, prefix_cot, w_out, lengths, adv_mask, patch_map):
    rows = saved.shape[1]
    width = saved.shape[3]
    heads_here = width // HD
    scale = 1.0 / math.sqrt(HD)
    live = lax.broadcasted_iota(jnp.int32, adv_mask.shape, 2) < lengths[:, :, None]
    resp_weight = jnp.sum(jnp.where(live, adv_mask, 0).astype(jnp.float32), axis=2) / MAXLEN
    group_weight = jnp.sum(resp_weight)
    share = lax.psum_scatter(
        (group_weight * prefix_cot[0, 0].astype(jnp.float32)).astype(jnp.bfloat16),
        "resp",
        scatter_dimension=0,
        tiled=True,
    )
    total = lax.all_gather(share, "resp", axis=0, tiled=True)
    cot_rows = jnp.take(total, patch_map[0, 0], axis=0)
    grad_out = lax.dot_general(
        cot_rows, w_out, (((1,), (1,)), ((), ())), preferred_element_type=jnp.float32
    ).astype(jnp.bfloat16)
    query = saved[0, :, 0, :].reshape(rows, heads_here, HD)
    keys = saved[0, :, 1, :].reshape(rows, heads_here, HD)
    values = saved[0, :, 2, :].reshape(rows, heads_here, HD)
    grad = grad_out.reshape(rows, heads_here, HD)
    key_value = saved[0, :, 1:, :].reshape(rows, 2 * width)
    piece = lax.all_gather(key_value, "blk", axis=0, tiled=True)
    top = jnp.full((heads_here, rows), -1e30, jnp.float32)
    count = piece.shape[0]
    key_part = piece[:, :width].reshape(count, heads_here, HD)
    value_part = piece[:, width:].reshape(count, heads_here, HD)
    score = jnp.einsum("qhd,khd->hqk", query, key_part, preferred_element_type=jnp.float32) * scale
    new_top = jnp.maximum(top, jnp.max(score, axis=2))
    expo = jnp.exp(score - new_top[:, :, None])
    row_total = jnp.sum(expo, axis=2)
    accum = jnp.einsum(
        "hqk,khd->hqd", expo.astype(jnp.bfloat16), value_part, preferred_element_type=jnp.float32
    )
    top, row_total, accum = (new_top, row_total, accum)
    output = (accum / row_total[:, :, None]).astype(jnp.bfloat16)
    log_total = top + jnp.log(row_total)
    delta = jnp.einsum("qhd,hqd->hq", grad, output, preferred_element_type=jnp.float32)
    packed = jnp.concatenate([saved[0], grad_out[:, None, :]], axis=1).reshape(rows, 4 * width)
    stats = jnp.concatenate([log_total, delta], axis=0).T
    block = lax.all_gather(packed.astype(jnp.float32), "blk", axis=0, tiled=True).astype(
        jnp.bfloat16
    )
    stat_block = lax.all_gather(stats, "blk", axis=0, tiled=True)
    count = block.shape[0]
    far_q = block[:, :width].reshape(count, heads_here, HD)
    far_k = block[:, width : 2 * width].reshape(count, heads_here, HD)
    far_v = block[:, 2 * width : 3 * width].reshape(count, heads_here, HD)
    far_g = block[:, 3 * width :].reshape(count, heads_here, HD)
    far_log = stat_block[:, :heads_here].T
    far_delta = stat_block[:, heads_here:].T
    near_prob, near_ds = score_pair(query, grad, log_total, delta, far_k, far_v, scale)
    grad_q = jnp.einsum("hqk,khd->hqd", near_ds, far_k, preferred_element_type=jnp.float32) * scale
    far_prob, far_ds = score_pair(far_q, far_g, far_log, far_delta, keys, values, scale)
    grad_k = jnp.einsum("hqk,qhd->khd", far_ds, far_q, preferred_element_type=jnp.float32) * scale
    grad_v = jnp.einsum("hqk,qhd->khd", far_prob, far_g, preferred_element_type=jnp.float32)
    grad_q, grad_k, grad_v = (grad_q, grad_k, grad_v)
    grad_k = grad_k.reshape(rows, width)
    grad_v = grad_v.reshape(rows, width)
    grad_q = grad_q.transpose(1, 0, 2).reshape(rows, width)
    result = jnp.stack([grad_q, grad_k, grad_v], axis=1).astype(jnp.bfloat16)
    return result[None]


def kernel(
    n_blk,
    n_resp,
    saved,
    cot,
    w_hbm,
    lengths,
    adv,
    pmap,
    out,
    w_out,
    qkv_t,
    grad_t,
    got,
    got_cot,
    weight,
    got_weight,
    prob,
    fwd_out,
    res,
    back,
    w_sem,
    own_sem,
    cot_sems,
    weight_sems,
    qkv_sems,
    grad_sems,
    back_sems,
):
    _, rows, width = saved.shape
    hp = got.shape[1]
    share = hp * HD
    scale = 1.0 / math.sqrt(HD)
    me = lax.axis_index("blk")
    group = lax.axis_index("resp")
    peers = [lax.rem(me + k, n_blk) for k in range(1, n_blk)]
    partners = [lax.rem(group + k, n_resp) for k in range(1, n_resp)]

    barrier = pltpu.get_barrier_semaphore()
    for peer in peers:
        pl.semaphore_signal(barrier, 1, device_id={"blk": peer}, device_id_type=MESH)
    for partner in partners:
        pl.semaphore_signal(barrier, 1, device_id={"resp": partner}, device_id_type=MESH)
    w_copy = pltpu.make_async_copy(w_hbm, w_out, w_sem)
    w_copy.start()

    def remote(src, dst, sems, index, axis, target):
        return pltpu.make_async_remote_copy(
            src_ref=src,
            dst_ref=dst,
            send_sem=sems.at[(0, *index)],
            recv_sem=sems.at[(1, *index)],
            device_id={axis: target},
            device_id_type=MESH,
        )

    def feature(owner, a):
        return pl.ds(pl.multiple_of(owner * share + a * HD, 16), HD)

    def patches(owner):
        return pl.ds(pl.multiple_of(owner * rows, 128), rows)

    for t in range(3):
        for c in range(0, width, 128):
            qkv_t[t, c : c + 128, :] = saved[t, :, c : c + 128].T

    token = lax.broadcasted_iota(jnp.int32, (1, adv.shape[1]), 1)
    own_weight = jnp.zeros((1, 1), jnp.float32)
    for r in range(adv.shape[0]):
        live = jnp.where(token < lengths[0, r], adv[r : r + 1, :], 0).astype(jnp.float32)
        own_weight += jnp.sum(live, axis=1, keepdims=True) / MAXLEN
    weight[...] = jnp.broadcast_to(own_weight, weight.shape)

    pl.semaphore_wait(barrier, len(peers) + len(partners))

    qkv_copies = [
        [
            remote(
                qkv_t.at[:, feature(peer, a), :],
                got.at[pl.ds(0, 3), a, :, patches(me)],
                qkv_sems,
                (a, k),
                "blk",
                peer,
            )
            for k, peer in enumerate(peers)
        ]
        for a in range(hp)
    ]
    cot_copies = [
        remote(cot, got_cot.at[k], cot_sems, (k,), "resp", partner)
        for k, partner in enumerate(partners)
    ]
    weight_copies = [
        remote(weight, got_weight.at[k], weight_sems, (k,), "resp", partner)
        for k, partner in enumerate(partners)
    ]
    own_qkv = [
        pltpu.make_async_copy(
            qkv_t.at[:, feature(me, a), :],
            got.at[pl.ds(0, 3), a, :, patches(me)],
            own_sem.at[0, a],
        )
        for a in range(hp)
    ]
    for copy in weight_copies + cot_copies + qkv_copies[0] + own_qkv:
        copy.start()
    for copies in qkv_copies[1:]:
        for copy in copies:
            copy.start()

    for copy in weight_copies + cot_copies:
        copy.wait_recv()
    total = own_weight * cot[...].astype(jnp.float32)
    for k in range(len(partners)):
        total += got_weight[k, 0:1, 0:1] * got_cot[k].astype(jnp.float32)
    w_copy.wait()
    grad = lax.dot_general(
        w_out[...],
        total.astype(jnp.bfloat16),
        (((1,), (1,)), ((), ())),
        preferred_element_type=jnp.float32,
    ).astype(jnp.bfloat16)
    place = lax.broadcasted_iota(jnp.int32, (rows, rows), 0) == pmap[...]
    grad_t[...] = jnp.dot(
        grad, place.astype(jnp.bfloat16), preferred_element_type=jnp.float32
    ).astype(jnp.bfloat16)
    grad_copies = [
        [
            remote(
                grad_t.at[feature(peer, a), :],
                got.at[3, a, :, patches(me)],
                grad_sems,
                (a, k),
                "blk",
                peer,
            )
            for k, peer in enumerate(peers)
        ]
        for a in range(hp)
    ]
    own_grad = [
        pltpu.make_async_copy(
            grad_t.at[feature(me, a), :], got.at[3, a, :, patches(me)], own_sem.at[1, a]
        )
        for a in range(hp)
    ]
    for a in range(hp):
        for copy in grad_copies[a] + [own_grad[a]]:
            copy.start()

    for a in range(hp):
        for copy in qkv_copies[a]:
            copy.wait_recv()
        own_qkv[a].wait()
        score = (
            jnp.dot(got[1, a].T, got[0, a], preferred_element_type=jnp.float32) * scale
        )
        expo = jnp.exp(score - jnp.max(score, axis=0, keepdims=True))
        inverse = 1.0 / jnp.sum(expo, axis=0, keepdims=True)
        fwd_out[a] = (
            jnp.dot(got[2, a], expo.astype(jnp.bfloat16), preferred_element_type=jnp.float32)
            * inverse
        ).astype(jnp.bfloat16)
        prob[a] = expo * inverse

    back_copies = []
    own_back = []
    for a in range(hp):
        for copy in grad_copies[a]:
            copy.wait_recv()
        own_grad[a].wait()
        grad = got[3, a]
        delta = jnp.sum(
            grad.astype(jnp.float32) * fwd_out[a].astype(jnp.float32), axis=0, keepdims=True
        )
        dprob = jnp.dot(got[2, a].T, grad, preferred_element_type=jnp.float32)
        dscore = (prob[a] * (dprob - delta)).astype(jnp.bfloat16)
        res[a, 0] = (
            jnp.dot(got[1, a], dscore, preferred_element_type=jnp.float32) * scale
        ).astype(jnp.bfloat16)
        res[a, 1] = (
            lax.dot_general(
                got[0, a], dscore, (((1,), (1,)), ((), ())), preferred_element_type=jnp.float32
            )
            * scale
        ).astype(jnp.bfloat16)
        res[a, 2] = lax.dot_general(
            grad,
            prob[a].astype(jnp.bfloat16),
            (((1,), (1,)), ((), ())),
            preferred_element_type=jnp.float32,
        ).astype(jnp.bfloat16)
        for k, peer in enumerate(peers):
            back_copies.append(
                remote(
                    res.at[a, :, :, patches(peer)],
                    back.at[:, feature(me, a), :],
                    back_sems,
                    (a, k),
                    "blk",
                    peer,
                )
            )
            back_copies[-1].start()
        own_back.append(
            pltpu.make_async_copy(
                res.at[a, :, :, patches(me)], back.at[:, feature(me, a), :], own_sem.at[2, a]
            )
        )
        own_back[-1].start()

    for copy in back_copies:
        copy.wait_recv()
    for copy in own_back:
        copy.wait()
    for t in range(3):
        for c in range(0, width, 128):
            out[t, :, c : c + 128] = back[t, c : c + 128, :].T
    for copy in weight_copies + cot_copies + sum(qkv_copies + grad_copies, []) + back_copies:
        copy.wait_send()


def exchanged(n_blk, n_resp, saved, prefix_cot, w_out, lengths, adv_mask, patch_map):
    rows, width = saved.shape[1], saved.shape[3]
    model = w_out.shape[1]
    hp = width // HD // n_blk
    count = n_blk * rows
    bf16, f32 = jnp.bfloat16, jnp.float32
    vmem = pl.BlockSpec(memory_space=pltpu.VMEM)
    dma = pltpu.SemaphoreType.DMA
    result = pl.pallas_call(
        functools.partial(kernel, n_blk, n_resp),
        out_shape=jax.ShapeDtypeStruct((3, rows, width), bf16),
        in_specs=[
            vmem,
            vmem,
            pl.BlockSpec(memory_space=pl.ANY),
            pl.BlockSpec(memory_space=pltpu.SMEM),
            vmem,
            vmem,
        ],
        out_specs=vmem,
        scratch_shapes=[
            pltpu.VMEM((width, model), bf16),
            pltpu.VMEM((3, width, rows), bf16),
            pltpu.VMEM((width, rows), bf16),
            pltpu.VMEM((4, hp, HD, count), bf16),
            pltpu.VMEM((n_resp - 1, rows, model), bf16),
            pltpu.VMEM((8, 128), f32),
            pltpu.VMEM((n_resp - 1, 8, 128), f32),
            pltpu.VMEM((hp, count, count), f32),
            pltpu.VMEM((hp, HD, count), bf16),
            pltpu.VMEM((hp, 3, HD, count), bf16),
            pltpu.VMEM((3, width, rows), bf16),
            dma,
            dma((3, hp)),
            dma((2, n_resp - 1)),
            dma((2, n_resp - 1)),
            dma((2, hp, n_blk - 1)),
            dma((2, hp, n_blk - 1)),
            dma((2, hp, n_blk - 1)),
        ],
        compiler_params=pltpu.CompilerParams(
            collective_id=0, has_side_effects=True, vmem_limit_bytes=40 * 1024 * 1024
        ),
        name="prefix_backward",
    )(
        saved[0].transpose(1, 0, 2),
        prefix_cot[0, 0],
        w_out,
        lengths,
        adv_mask[0],
        patch_map[0],
    )
    return result.transpose(1, 0, 2)[None]


def shards(n_blk, n_resp, saved, *rest):
    rows, width = saved.shape[1], saved.shape[3]
    even = (width // HD) % n_blk == 0 and rows % 128 == 0 and width % 128 == 0
    if even and n_blk > 1 and n_resp > 1:
        return exchanged(n_blk, n_resp, saved, *rest)
    return gathered(saved, *rest)


def solution(mesh):
    in_specs = (
        P("dp", "blk", None, "resp"),
        P("dp", "resp", "blk", None),
        P("resp", None),
        P("dp", "resp"),
        P("dp", "resp", None),
        P("dp", "blk", None),
    )
    out_specs = P("dp", "blk", None, "resp")
    sizes = (mesh.shape["blk"], mesh.shape["resp"])
    return jax.shard_map(functools.partial(shards, *sizes), mesh=mesh, in_specs=in_specs, out_specs=out_specs, check_vma=False)
```

```python
import functools
import math

import jax
import jax.numpy as jnp
from jax import lax
from jax.experimental import pallas as pl
from jax.experimental.pallas import tpu as pltpu
from jax.sharding import PartitionSpec as P

HD = 80
MAXLEN = 512
MESH = pl.DeviceIdType.MESH


def score_pair(query, grad, log_total, delta, keys, values, scale):
    score = jnp.einsum("qhd,khd->hqk", query, keys, preferred_element_type=jnp.float32) * scale
    prob = jnp.exp(score - log_total[:, :, None])
    dprob = jnp.einsum("qhd,khd->hqk", grad, values, preferred_element_type=jnp.float32)
    dscore = (prob * (dprob - delta[:, :, None])).astype(jnp.bfloat16)
    return (prob.astype(jnp.bfloat16), dscore)


def gathered(saved, prefix_cot, w_out, lengths, adv_mask, patch_map):
    rows = saved.shape[1]
    width = saved.shape[3]
    heads_here = width // HD
    scale = 1.0 / math.sqrt(HD)
    live = lax.broadcasted_iota(jnp.int32, adv_mask.shape, 2) < lengths[:, :, None]
    resp_weight = jnp.sum(jnp.where(live, adv_mask, 0).astype(jnp.float32), axis=2) / MAXLEN
    group_weight = jnp.sum(resp_weight)
    share = lax.psum_scatter(
        (group_weight * prefix_cot[0, 0].astype(jnp.float32)).astype(jnp.bfloat16),
        "resp",
        scatter_dimension=0,
        tiled=True,
    )
    total = lax.all_gather(share, "resp", axis=0, tiled=True)
    cot_rows = jnp.take(total, patch_map[0, 0], axis=0)
    grad_out = lax.dot_general(
        cot_rows, w_out, (((1,), (1,)), ((), ())), preferred_element_type=jnp.float32
    ).astype(jnp.bfloat16)
    query = saved[0, :, 0, :].reshape(rows, heads_here, HD)
    keys = saved[0, :, 1, :].reshape(rows, heads_here, HD)
    values = saved[0, :, 2, :].reshape(rows, heads_here, HD)
    grad = grad_out.reshape(rows, heads_here, HD)
    key_value = saved[0, :, 1:, :].reshape(rows, 2 * width)
    piece = lax.all_gather(key_value, "blk", axis=0, tiled=True)
    top = jnp.full((heads_here, rows), -1e30, jnp.float32)
    count = piece.shape[0]
    key_part = piece[:, :width].reshape(count, heads_here, HD)
    value_part = piece[:, width:].reshape(count, heads_here, HD)
    score = jnp.einsum("qhd,khd->hqk", query, key_part, preferred_element_type=jnp.float32) * scale
    new_top = jnp.maximum(top, jnp.max(score, axis=2))
    expo = jnp.exp(score - new_top[:, :, None])
    row_total = jnp.sum(expo, axis=2)
    accum = jnp.einsum(
        "hqk,khd->hqd", expo.astype(jnp.bfloat16), value_part, preferred_element_type=jnp.float32
    )
    top, row_total, accum = (new_top, row_total, accum)
    output = (accum / row_total[:, :, None]).astype(jnp.bfloat16)
    log_total = top + jnp.log(row_total)
    delta = jnp.einsum("qhd,hqd->hq", grad, output, preferred_element_type=jnp.float32)
    packed = jnp.concatenate([saved[0], grad_out[:, None, :]], axis=1).reshape(rows, 4 * width)
    stats = jnp.concatenate([log_total, delta], axis=0).T
    block = lax.all_gather(packed.astype(jnp.float32), "blk", axis=0, tiled=True).astype(
        jnp.bfloat16
    )
    stat_block = lax.all_gather(stats, "blk", axis=0, tiled=True)
    count = block.shape[0]
    far_q = block[:, :width].reshape(count, heads_here, HD)
    far_k = block[:, width : 2 * width].reshape(count, heads_here, HD)
    far_v = block[:, 2 * width : 3 * width].reshape(count, heads_here, HD)
    far_g = block[:, 3 * width :].reshape(count, heads_here, HD)
    far_log = stat_block[:, :heads_here].T
    far_delta = stat_block[:, heads_here:].T
    near_prob, near_ds = score_pair(query, grad, log_total, delta, far_k, far_v, scale)
    grad_q = jnp.einsum("hqk,khd->hqd", near_ds, far_k, preferred_element_type=jnp.float32) * scale
    far_prob, far_ds = score_pair(far_q, far_g, far_log, far_delta, keys, values, scale)
    grad_k = jnp.einsum("hqk,qhd->khd", far_ds, far_q, preferred_element_type=jnp.float32) * scale
    grad_v = jnp.einsum("hqk,qhd->khd", far_prob, far_g, preferred_element_type=jnp.float32)
    grad_q, grad_k, grad_v = (grad_q, grad_k, grad_v)
    grad_k = grad_k.reshape(rows, width)
    grad_v = grad_v.reshape(rows, width)
    grad_q = grad_q.transpose(1, 0, 2).reshape(rows, width)
    result = jnp.stack([grad_q, grad_k, grad_v], axis=1).astype(jnp.bfloat16)
    return result[None]


def kernel(
    n_blk,
    n_resp,
    saved_hbm,
    cot_hbm,
    w_hbm,
    lengths_hbm,
    adv_hbm,
    pmap_hbm,
    out,
    saved,
    cot,
    w_out,
    lengths,
    adv,
    pmap,
    qkv_t,
    grad_t,
    got,
    got_cot,
    weight,
    got_weight,
    prob,
    fwd_out,
    res,
    back,
    load_sems,
    own_sem,
    cot_sems,
    weight_sems,
    qkv_sems,
    grad_sems,
    back_sems,
):
    _, rows, width = saved.shape
    hp = got.shape[1]
    share = hp * HD
    scale = 1.0 / math.sqrt(HD)
    me = lax.axis_index("blk")
    group = lax.axis_index("resp")
    peers = [lax.rem(me + k, n_blk) for k in range(1, n_blk)]
    partners = [lax.rem(group + k, n_resp) for k in range(1, n_resp)]

    barrier = pltpu.get_barrier_semaphore()
    for peer in peers:
        pl.semaphore_signal(barrier, 1, device_id={"blk": peer}, device_id_type=MESH)
    for partner in partners:
        pl.semaphore_signal(barrier, 1, device_id={"resp": partner}, device_id_type=MESH)
    pairs = [(saved_hbm.at[t], saved.at[t]) for t in range(3)]
    pairs += [(lengths_hbm, lengths), (adv_hbm, adv), (pmap_hbm, pmap)]
    pairs += [(cot_hbm, cot), (w_hbm, w_out)]
    loads = [
        pltpu.make_async_copy(src, dst, load_sems.at[n]) for n, (src, dst) in enumerate(pairs)
    ]
    for load in loads:
        load.start()

    def remote(src, dst, sems, index, axis, target):
        return pltpu.make_async_remote_copy(
            src_ref=src,
            dst_ref=dst,
            send_sem=sems.at[(0, *index)],
            recv_sem=sems.at[(1, *index)],
            device_id={axis: target},
            device_id_type=MESH,
        )

    def feature(owner, a):
        return pl.ds(pl.multiple_of(owner * share + a * HD, 16), HD)

    def patches(owner):
        return pl.ds(pl.multiple_of(owner * rows, 128), rows)

    for t in range(3):
        loads[t].wait()
        for c in range(0, width, 128):
            qkv_t[t, c : c + 128, :] = saved[t, :, c : c + 128].T

    for load in loads[3:6]:
        load.wait()
    token = lax.broadcasted_iota(jnp.int32, (1, adv.shape[1]), 1)
    own_weight = jnp.zeros((1, 1), jnp.float32)
    for r in range(adv.shape[0]):
        live = jnp.where(token < lengths[0:1, r : r + 1], adv[r : r + 1, :], 0).astype(jnp.float32)
        own_weight += jnp.sum(live, axis=1, keepdims=True) / MAXLEN
    weight[...] = jnp.broadcast_to(own_weight, weight.shape)

    pl.semaphore_wait(barrier, len(peers) + len(partners))

    qkv_copies = [
        [
            remote(
                qkv_t.at[:, feature(peer, a), :],
                got.at[pl.ds(0, 3), a, :, patches(me)],
                qkv_sems,
                (a, k),
                "blk",
                peer,
            )
            for k, peer in enumerate(peers)
        ]
        for a in range(hp)
    ]
    cot_copies = [
        remote(cot_hbm, got_cot.at[k], cot_sems, (k,), "resp", partner)
        for k, partner in enumerate(partners)
    ]
    weight_copies = [
        remote(weight, got_weight.at[k], weight_sems, (k,), "resp", partner)
        for k, partner in enumerate(partners)
    ]
    own_qkv = [
        pltpu.make_async_copy(
            qkv_t.at[:, feature(me, a), :],
            got.at[pl.ds(0, 3), a, :, patches(me)],
            own_sem.at[0, a],
        )
        for a in range(hp)
    ]
    for copy in weight_copies + cot_copies + qkv_copies[0] + own_qkv:
        copy.start()
    for copies in qkv_copies[1:]:
        for copy in copies:
            copy.start()

    for copy in weight_copies + cot_copies:
        copy.wait_recv()
    for load in loads[6:]:
        load.wait()
    total = own_weight * cot[...].astype(jnp.float32)
    for k in range(len(partners)):
        total += got_weight[k, 0:1, 0:1] * got_cot[k].astype(jnp.float32)
    grad = lax.dot_general(
        w_out[...],
        total.astype(jnp.bfloat16),
        (((1,), (1,)), ((), ())),
        preferred_element_type=jnp.float32,
    ).astype(jnp.bfloat16)
    place = lax.broadcasted_iota(jnp.int32, (rows, rows), 0) == pmap[...]
    grad_t[...] = jnp.dot(
        grad, place.astype(jnp.bfloat16), preferred_element_type=jnp.float32
    ).astype(jnp.bfloat16)
    grad_copies = [
        [
            remote(
                grad_t.at[feature(peer, a), :],
                got.at[3, a, :, patches(me)],
                grad_sems,
                (a, k),
                "blk",
                peer,
            )
            for k, peer in enumerate(peers)
        ]
        for a in range(hp)
    ]
    own_grad = [
        pltpu.make_async_copy(
            grad_t.at[feature(me, a), :], got.at[3, a, :, patches(me)], own_sem.at[1, a]
        )
        for a in range(hp)
    ]
    for a in range(hp):
        for copy in grad_copies[a] + [own_grad[a]]:
            copy.start()

    for a in range(hp):
        for copy in qkv_copies[a]:
            copy.wait_recv()
        own_qkv[a].wait()
        score = (
            jnp.dot(got[1, a].T, got[0, a], preferred_element_type=jnp.float32) * scale
        )
        expo = jnp.exp(score - jnp.max(score, axis=0, keepdims=True))
        inverse = 1.0 / jnp.sum(expo, axis=0, keepdims=True)
        fwd_out[a] = (
            jnp.dot(got[2, a], expo.astype(jnp.bfloat16), preferred_element_type=jnp.float32)
            * inverse
        ).astype(jnp.bfloat16)
        prob[a] = expo * inverse

    back_copies = []
    own_back = []
    for a in range(hp):
        for copy in grad_copies[a]:
            copy.wait_recv()
        own_grad[a].wait()
        grad = got[3, a]
        delta = jnp.sum(
            grad.astype(jnp.float32) * fwd_out[a].astype(jnp.float32), axis=0, keepdims=True
        )
        dprob = jnp.dot(got[2, a].T, grad, preferred_element_type=jnp.float32)
        dscore = (prob[a] * (dprob - delta)).astype(jnp.bfloat16)
        res[a, 0] = (
            jnp.dot(got[1, a], dscore, preferred_element_type=jnp.float32) * scale
        ).astype(jnp.bfloat16)
        res[a, 1] = (
            lax.dot_general(
                got[0, a], dscore, (((1,), (1,)), ((), ())), preferred_element_type=jnp.float32
            )
            * scale
        ).astype(jnp.bfloat16)
        res[a, 2] = lax.dot_general(
            grad,
            prob[a].astype(jnp.bfloat16),
            (((1,), (1,)), ((), ())),
            preferred_element_type=jnp.float32,
        ).astype(jnp.bfloat16)
        for k, peer in enumerate(peers):
            back_copies.append(
                remote(
                    res.at[a, :, :, patches(peer)],
                    back.at[:, feature(me, a), :],
                    back_sems,
                    (a, k),
                    "blk",
                    peer,
                )
            )
            back_copies[-1].start()
        own_back.append(
            pltpu.make_async_copy(
                res.at[a, :, :, patches(me)], back.at[:, feature(me, a), :], own_sem.at[2, a]
            )
        )
        own_back[-1].start()

    for copy in back_copies:
        copy.wait_recv()
    for copy in own_back:
        copy.wait()
    for t in range(3):
        for c in range(0, width, 128):
            out[t, :, c : c + 128] = back[t, c : c + 128, :].T
    for copy in weight_copies + cot_copies + sum(qkv_copies + grad_copies, []) + back_copies:
        copy.wait_send()


def exchanged(n_blk, n_resp, saved, prefix_cot, w_out, lengths, adv_mask, patch_map):
    rows, width = saved.shape[1], saved.shape[3]
    model = w_out.shape[1]
    hp = width // HD // n_blk
    count = n_blk * rows
    bf16, f32 = jnp.bfloat16, jnp.float32
    dma = pltpu.SemaphoreType.DMA
    result = pl.pallas_call(
        functools.partial(kernel, n_blk, n_resp),
        out_shape=jax.ShapeDtypeStruct((3, rows, width), bf16),
        in_specs=[pl.BlockSpec(memory_space=pltpu.HBM)] * 6,
        out_specs=pl.BlockSpec(memory_space=pltpu.VMEM),
        scratch_shapes=[
            pltpu.VMEM((3, rows, width), bf16),
            pltpu.VMEM((rows, model), bf16),
            pltpu.VMEM((width, model), bf16),
            pltpu.VMEM(lengths.shape, jnp.int32),
            pltpu.VMEM(adv_mask.shape[1:], jnp.int32),
            pltpu.VMEM(patch_map.shape[1:], jnp.int32),
            pltpu.VMEM((3, width, rows), bf16),
            pltpu.VMEM((width, rows), bf16),
            pltpu.VMEM((4, hp, HD, count), bf16),
            pltpu.VMEM((n_resp - 1, rows, model), bf16),
            pltpu.VMEM((8, 128), f32),
            pltpu.VMEM((n_resp - 1, 8, 128), f32),
            pltpu.VMEM((hp, count, count), f32),
            pltpu.VMEM((hp, HD, count), bf16),
            pltpu.VMEM((hp, 3, HD, count), bf16),
            pltpu.VMEM((3, width, rows), bf16),
            dma((8,)),
            dma((3, hp)),
            dma((2, n_resp - 1)),
            dma((2, n_resp - 1)),
            dma((2, hp, n_blk - 1)),
            dma((2, hp, n_blk - 1)),
            dma((2, hp, n_blk - 1)),
        ],
        compiler_params=pltpu.CompilerParams(
            collective_id=0, has_side_effects=True, vmem_limit_bytes=40 * 1024 * 1024
        ),
        name="prefix_backward",
    )(
        *(
            pltpu.with_memory_space_constraint(array, pltpu.HBM)
            for array in (
                saved[0].transpose(1, 0, 2),
                prefix_cot[0, 0],
                w_out,
                lengths,
                adv_mask[0],
                patch_map[0],
            )
        )
    )
    return result.transpose(1, 0, 2)[None]


def shards(n_blk, n_resp, saved, *rest):
    rows, width = saved.shape[1], saved.shape[3]
    even = (width // HD) % n_blk == 0 and rows % 128 == 0 and width % 128 == 0
    if even and n_blk > 1 and n_resp > 1:
        return exchanged(n_blk, n_resp, saved, *rest)
    return gathered(saved, *rest)


def solution(mesh):
    in_specs = (
        P("dp", "blk", None, "resp"),
        P("dp", "resp", "blk", None),
        P("resp", None),
        P("dp", "resp"),
        P("dp", "resp", None),
        P("dp", "blk", None),
    )
    out_specs = P("dp", "blk", None, "resp")
    sizes = (mesh.shape["blk"], mesh.shape["resp"])
    return jax.shard_map(functools.partial(shards, *sizes), mesh=mesh, in_specs=in_specs, out_specs=out_specs, check_vma=False)
```

```python
import functools
import math

import jax
import jax.numpy as jnp
from jax import lax
from jax.experimental import pallas as pl
from jax.experimental.pallas import tpu as pltpu
from jax.sharding import PartitionSpec as P

HD = 80
MAXLEN = 512
MESH = pl.DeviceIdType.MESH


def score_pair(query, grad, log_total, delta, keys, values, scale):
    score = jnp.einsum("qhd,khd->hqk", query, keys, preferred_element_type=jnp.float32) * scale
    prob = jnp.exp(score - log_total[:, :, None])
    dprob = jnp.einsum("qhd,khd->hqk", grad, values, preferred_element_type=jnp.float32)
    dscore = (prob * (dprob - delta[:, :, None])).astype(jnp.bfloat16)
    return (prob.astype(jnp.bfloat16), dscore)


def gathered(saved, prefix_cot, w_out, lengths, adv_mask, patch_map):
    rows = saved.shape[1]
    width = saved.shape[3]
    heads_here = width // HD
    scale = 1.0 / math.sqrt(HD)
    live = lax.broadcasted_iota(jnp.int32, adv_mask.shape, 2) < lengths[:, :, None]
    resp_weight = jnp.sum(jnp.where(live, adv_mask, 0).astype(jnp.float32), axis=2) / MAXLEN
    group_weight = jnp.sum(resp_weight)
    share = lax.psum_scatter(
        (group_weight * prefix_cot[0, 0].astype(jnp.float32)).astype(jnp.bfloat16),
        "resp",
        scatter_dimension=0,
        tiled=True,
    )
    total = lax.all_gather(share, "resp", axis=0, tiled=True)
    cot_rows = jnp.take(total, patch_map[0, 0], axis=0)
    grad_out = lax.dot_general(
        cot_rows, w_out, (((1,), (1,)), ((), ())), preferred_element_type=jnp.float32
    ).astype(jnp.bfloat16)
    query = saved[0, :, 0, :].reshape(rows, heads_here, HD)
    keys = saved[0, :, 1, :].reshape(rows, heads_here, HD)
    values = saved[0, :, 2, :].reshape(rows, heads_here, HD)
    grad = grad_out.reshape(rows, heads_here, HD)
    key_value = saved[0, :, 1:, :].reshape(rows, 2 * width)
    piece = lax.all_gather(key_value, "blk", axis=0, tiled=True)
    top = jnp.full((heads_here, rows), -1e30, jnp.float32)
    count = piece.shape[0]
    key_part = piece[:, :width].reshape(count, heads_here, HD)
    value_part = piece[:, width:].reshape(count, heads_here, HD)
    score = jnp.einsum("qhd,khd->hqk", query, key_part, preferred_element_type=jnp.float32) * scale
    new_top = jnp.maximum(top, jnp.max(score, axis=2))
    expo = jnp.exp(score - new_top[:, :, None])
    row_total = jnp.sum(expo, axis=2)
    accum = jnp.einsum(
        "hqk,khd->hqd", expo.astype(jnp.bfloat16), value_part, preferred_element_type=jnp.float32
    )
    top, row_total, accum = (new_top, row_total, accum)
    output = (accum / row_total[:, :, None]).astype(jnp.bfloat16)
    log_total = top + jnp.log(row_total)
    delta = jnp.einsum("qhd,hqd->hq", grad, output, preferred_element_type=jnp.float32)
    packed = jnp.concatenate([saved[0], grad_out[:, None, :]], axis=1).reshape(rows, 4 * width)
    stats = jnp.concatenate([log_total, delta], axis=0).T
    block = lax.all_gather(packed.astype(jnp.float32), "blk", axis=0, tiled=True).astype(
        jnp.bfloat16
    )
    stat_block = lax.all_gather(stats, "blk", axis=0, tiled=True)
    count = block.shape[0]
    far_q = block[:, :width].reshape(count, heads_here, HD)
    far_k = block[:, width : 2 * width].reshape(count, heads_here, HD)
    far_v = block[:, 2 * width : 3 * width].reshape(count, heads_here, HD)
    far_g = block[:, 3 * width :].reshape(count, heads_here, HD)
    far_log = stat_block[:, :heads_here].T
    far_delta = stat_block[:, heads_here:].T
    near_prob, near_ds = score_pair(query, grad, log_total, delta, far_k, far_v, scale)
    grad_q = jnp.einsum("hqk,khd->hqd", near_ds, far_k, preferred_element_type=jnp.float32) * scale
    far_prob, far_ds = score_pair(far_q, far_g, far_log, far_delta, keys, values, scale)
    grad_k = jnp.einsum("hqk,qhd->khd", far_ds, far_q, preferred_element_type=jnp.float32) * scale
    grad_v = jnp.einsum("hqk,qhd->khd", far_prob, far_g, preferred_element_type=jnp.float32)
    grad_q, grad_k, grad_v = (grad_q, grad_k, grad_v)
    grad_k = grad_k.reshape(rows, width)
    grad_v = grad_v.reshape(rows, width)
    grad_q = grad_q.transpose(1, 0, 2).reshape(rows, width)
    result = jnp.stack([grad_q, grad_k, grad_v], axis=1).astype(jnp.bfloat16)
    return result[None]


def kernel(
    n_blk,
    n_resp,
    saved_hbm,
    cot_hbm,
    w_hbm,
    lengths_hbm,
    adv_hbm,
    pmap_hbm,
    out,
    saved,
    cot,
    w_out,
    lengths,
    adv,
    pmap,
    qkv_t,
    grad_t,
    got,
    got_cot,
    weight,
    got_weight,
    prob,
    fwd_out,
    res,
    back,
    load_sems,
    own_sem,
    cot_sems,
    weight_sems,
    qkv_sems,
    grad_sems,
    back_sems,
):
    _, rows, width = saved.shape
    hp = got.shape[1]
    share = hp * HD
    scale = 1.0 / math.sqrt(HD)
    me = lax.axis_index("blk")
    group = lax.axis_index("resp")
    peers = [lax.rem(me + k, n_blk) for k in range(1, n_blk)]
    partners = [lax.rem(group + k, n_resp) for k in range(1, n_resp)]

    barrier = pltpu.get_barrier_semaphore()
    for peer in peers:
        pl.semaphore_signal(barrier, 1, device_id={"blk": peer}, device_id_type=MESH)
    for partner in partners:
        pl.semaphore_signal(barrier, 1, device_id={"resp": partner}, device_id_type=MESH)
    pairs = [(saved_hbm.at[t], saved.at[t]) for t in range(3)]
    pairs += [(lengths_hbm, lengths), (adv_hbm, adv), (pmap_hbm, pmap)]
    pairs += [(cot_hbm, cot), (w_hbm, w_out)]
    loads = [
        pltpu.make_async_copy(src, dst, load_sems.at[n]) for n, (src, dst) in enumerate(pairs)
    ]
    for load in loads:
        load.start()

    def remote(src, dst, sems, index, axis, target):
        return pltpu.make_async_remote_copy(
            src_ref=src,
            dst_ref=dst,
            send_sem=sems.at[(0, *index)],
            recv_sem=sems.at[(1, *index)],
            device_id={axis: target},
            device_id_type=MESH,
        )

    def feature(owner, a):
        return pl.ds(pl.multiple_of(owner * share + a * HD, 16), HD)

    def patches(owner):
        return pl.ds(pl.multiple_of(owner * rows, 128), rows)

    for t in range(3):
        loads[t].wait()
        for c in range(0, width, 128):
            qkv_t[t, c : c + 128, :] = saved[t, :, c : c + 128].T

    for load in loads[3:6]:
        load.wait()
    token = lax.broadcasted_iota(jnp.int32, (1, adv.shape[1]), 1)
    own_weight = jnp.zeros((1, 1), jnp.float32)
    for r in range(adv.shape[0]):
        live = jnp.where(token < lengths[0:1, r : r + 1], adv[r : r + 1, :], 0).astype(jnp.float32)
        own_weight += jnp.sum(live, axis=1, keepdims=True) / MAXLEN
    weight[...] = jnp.broadcast_to(own_weight, weight.shape)

    pl.semaphore_wait(barrier, len(peers) + len(partners))

    qkv_copies = [
        [
            remote(
                qkv_t.at[:, feature(peer, a), :],
                got.at[pl.ds(0, 3), a, :, patches(me)],
                qkv_sems,
                (a, k),
                "blk",
                peer,
            )
            for k, peer in enumerate(peers)
        ]
        for a in range(hp)
    ]
    cot_copies = [
        remote(cot_hbm, got_cot.at[k], cot_sems, (k,), "resp", partner)
        for k, partner in enumerate(partners)
    ]
    weight_copies = [
        remote(weight, got_weight.at[k], weight_sems, (k,), "resp", partner)
        for k, partner in enumerate(partners)
    ]
    own_qkv = [
        pltpu.make_async_copy(
            qkv_t.at[:, feature(me, a), :],
            got.at[pl.ds(0, 3), a, :, patches(me)],
            own_sem.at[0, a],
        )
        for a in range(hp)
    ]
    for copy in weight_copies + cot_copies + qkv_copies[0] + own_qkv:
        copy.start()
    for copies in qkv_copies[1:]:
        for copy in copies:
            copy.start()

    for copy in weight_copies + cot_copies:
        copy.wait_recv()
    for load in loads[6:]:
        load.wait()
    total = own_weight * cot[...].astype(jnp.float32)
    for k in range(len(partners)):
        total += got_weight[k, 0:1, 0:1] * got_cot[k].astype(jnp.float32)
    grad = lax.dot_general(
        w_out[...],
        total.astype(jnp.bfloat16),
        (((1,), (1,)), ((), ())),
        preferred_element_type=jnp.float32,
    ).astype(jnp.bfloat16)
    place = lax.broadcasted_iota(jnp.int32, (rows, rows), 0) == pmap[...]
    grad_t[...] = jnp.dot(
        grad, place.astype(jnp.bfloat16), preferred_element_type=jnp.float32
    ).astype(jnp.bfloat16)
    grad_copies = [
        [
            remote(
                grad_t.at[feature(peer, a), :],
                got.at[3, a, :, patches(me)],
                grad_sems,
                (a, k),
                "blk",
                peer,
            )
            for k, peer in enumerate(peers)
        ]
        for a in range(hp)
    ]
    own_grad = [
        pltpu.make_async_copy(
            grad_t.at[feature(me, a), :], got.at[3, a, :, patches(me)], own_sem.at[1, a]
        )
        for a in range(hp)
    ]
    for a in range(hp):
        for copy in grad_copies[a] + [own_grad[a]]:
            copy.start()

    for a in range(hp):
        for copy in qkv_copies[a]:
            copy.wait_recv()
        own_qkv[a].wait()
        score = (
            jnp.dot(got[1, a].T, got[0, a], preferred_element_type=jnp.float32) * scale
        )
        expo = jnp.exp(score - jnp.max(score, axis=0, keepdims=True))
        inverse = 1.0 / jnp.sum(expo, axis=0, keepdims=True)
        fwd_out[a] = (
            jnp.dot(got[2, a], expo.astype(jnp.bfloat16), preferred_element_type=jnp.float32)
            * inverse
        ).astype(jnp.bfloat16)
        prob[a] = expo * inverse

    back_copies = []
    own_back = []

    def give_back(a, first, size):
        for k, peer in enumerate(peers):
            back_copies.append(
                remote(
                    res.at[a, pl.ds(first, size), :, patches(peer)],
                    back.at[pl.ds(first, size), feature(me, a), :],
                    back_sems,
                    (first // 2, a, k),
                    "blk",
                    peer,
                )
            )
            back_copies[-1].start()
        own_back.append(
            pltpu.make_async_copy(
                res.at[a, pl.ds(first, size), :, patches(me)], back.at[pl.ds(first, size), feature(me, a), :], own_sem.at[2 + first // 2, a]
            )
        )
        own_back[-1].start()

    for a in range(hp):
        for copy in grad_copies[a]:
            copy.wait_recv()
        own_grad[a].wait()
        grad = got[3, a]
        res[a, 2] = lax.dot_general(
            grad,
            prob[a].astype(jnp.bfloat16),
            (((1,), (1,)), ((), ())),
            preferred_element_type=jnp.float32,
        ).astype(jnp.bfloat16)
        give_back(a, 2, 1)
        delta = jnp.sum(
            grad.astype(jnp.float32) * fwd_out[a].astype(jnp.float32), axis=0, keepdims=True
        )
        dprob = jnp.dot(got[2, a].T, grad, preferred_element_type=jnp.float32)
        dscore = (prob[a] * (dprob - delta)).astype(jnp.bfloat16)
        res[a, 0] = (
            jnp.dot(got[1, a], dscore, preferred_element_type=jnp.float32) * scale
        ).astype(jnp.bfloat16)
        res[a, 1] = (
            lax.dot_general(
                got[0, a], dscore, (((1,), (1,)), ((), ())), preferred_element_type=jnp.float32
            )
            * scale
        ).astype(jnp.bfloat16)
        give_back(a, 0, 2)

    for copy in back_copies:
        copy.wait_recv()
    for copy in own_back:
        copy.wait()
    for t in range(3):
        for c in range(0, width, 128):
            out[t, :, c : c + 128] = back[t, c : c + 128, :].T
    for copy in weight_copies + cot_copies + sum(qkv_copies + grad_copies, []) + back_copies:
        copy.wait_send()


def exchanged(n_blk, n_resp, saved, prefix_cot, w_out, lengths, adv_mask, patch_map):
    rows, width = saved.shape[1], saved.shape[3]
    model = w_out.shape[1]
    hp = width // HD // n_blk
    count = n_blk * rows
    bf16, f32 = jnp.bfloat16, jnp.float32
    dma = pltpu.SemaphoreType.DMA
    result = pl.pallas_call(
        functools.partial(kernel, n_blk, n_resp),
        out_shape=jax.ShapeDtypeStruct((3, rows, width), bf16),
        in_specs=[pl.BlockSpec(memory_space=pltpu.HBM)] * 6,
        out_specs=pl.BlockSpec(memory_space=pltpu.VMEM),
        scratch_shapes=[
            pltpu.VMEM((3, rows, width), bf16),
            pltpu.VMEM((rows, model), bf16),
            pltpu.VMEM((width, model), bf16),
            pltpu.VMEM(lengths.shape, jnp.int32),
            pltpu.VMEM(adv_mask.shape[1:], jnp.int32),
            pltpu.VMEM(patch_map.shape[1:], jnp.int32),
            pltpu.VMEM((3, width, rows), bf16),
            pltpu.VMEM((width, rows), bf16),
            pltpu.VMEM((4, hp, HD, count), bf16),
            pltpu.VMEM((n_resp - 1, rows, model), bf16),
            pltpu.VMEM((8, 128), f32),
            pltpu.VMEM((n_resp - 1, 8, 128), f32),
            pltpu.VMEM((hp, count, count), f32),
            pltpu.VMEM((hp, HD, count), bf16),
            pltpu.VMEM((hp, 3, HD, count), bf16),
            pltpu.VMEM((3, width, rows), bf16),
            dma((8,)),
            dma((4, hp)),
            dma((2, n_resp - 1)),
            dma((2, n_resp - 1)),
            dma((2, hp, n_blk - 1)),
            dma((2, hp, n_blk - 1)),
            dma((2, 2, hp, n_blk - 1)),
        ],
        compiler_params=pltpu.CompilerParams(
            collective_id=0, has_side_effects=True, vmem_limit_bytes=40 * 1024 * 1024
        ),
        name="prefix_backward",
    )(
        *(
            pltpu.with_memory_space_constraint(array, pltpu.HBM)
            for array in (
                saved[0].transpose(1, 0, 2),
                prefix_cot[0, 0],
                w_out,
                lengths,
                adv_mask[0],
                patch_map[0],
            )
        )
    )
    return result.transpose(1, 0, 2)[None]


def shards(n_blk, n_resp, saved, *rest):
    rows, width = saved.shape[1], saved.shape[3]
    even = (width // HD) % n_blk == 0 and rows % 128 == 0 and width % 128 == 0
    if even and n_blk > 1 and n_resp > 1:
        return exchanged(n_blk, n_resp, saved, *rest)
    return gathered(saved, *rest)


def solution(mesh):
    in_specs = (
        P("dp", "blk", None, "resp"),
        P("dp", "resp", "blk", None),
        P("resp", None),
        P("dp", "resp"),
        P("dp", "resp", None),
        P("dp", "blk", None),
    )
    out_specs = P("dp", "blk", None, "resp")
    sizes = (mesh.shape["blk"], mesh.shape["resp"])
    return jax.shard_map(functools.partial(shards, *sizes), mesh=mesh, in_specs=in_specs, out_specs=out_specs, check_vma=False)
```
